32 devices in a mesh: row: 4 (over x, core), col: 8 (over z, y).
Axes of the slice: x: 2, y: 2, z: 4, core: 2. Of those that a mesh axis runs over, the one named last changes fastest.
Arguments:
- row_records: bfloat16 [8, 1024, 384], P('row', 'col'), may hold values from -6 to 6
- row_valid: int32 [8, 1024], P('row', 'col'), may hold values 0 or 1
- col_records: bfloat16 [8, 512, 384], P('col', 'row'), may hold values from -6 to 6
- col_valid: int32 [8, 512], P('col', 'row'), may hold values 0 or 1
Outputs:
- correlation: float32 [65, 512, 1024], P(None, 'row', 'col')
The draws below stay inside these ranges and needn't reach their ends.
All inputs are finite; a program needn't handle non-finite values. No bound on the sum of `row_valid` or of `col_valid` on one device may be relied on, other than what follows from the above.
Results may differ from the reference program's by a relative error of at most 0.0003.
Values may be sent and summed in bfloat16 or wider, within the bound.
A program may use at most 128 MiB of HBM per device.

```python
import jax
import jax.numpy as jnp
from jax import lax

RC = 128
SAMPLES = 384
LAG = 32
STEPS = 4
WB = 1
NWIN = 8
NR = 1024
NC = 512
N_COL = 8


def place_ends(result, key, smallest, high):
    spot = [jax.random.randint(jax.random.fold_in(key, axis), (), 0, length) for axis, length in enumerate(result.shape)]
    longest = result.shape.index(max(result.shape))
    neighbour = spot[:longest] + [(spot[longest] + 1) % result.shape[longest]] + spot[longest + 1:]
    return result.at[tuple(spot)].set(smallest).at[tuple(neighbour)].set(high)


def block_scale(stream_key, dims, split, smallest, largest):
    def one(axis_at, parts):
        draws = jax.random.uniform(jax.random.fold_in(jax.random.fold_in(stream_key, 6), axis_at), (parts,), jnp.float32, smallest / len(split), largest / len(split))
        return jnp.repeat(jnp.exp(draws), dims[axis_at] // parts).reshape((-1,) + (1,) * (len(dims) - axis_at - 1))

    factor_of = one(*split[0])
    for cut in split[1:]:
        factor_of = factor_of * one(*cut)
    return factor_of


def noise(stream_key, dims, spread, bound, split=(), kind=jnp.bfloat16):
    values = jax.random.normal(stream_key, dims, jnp.float32) * spread
    if len(split) > 0:
        values = block_scale(stream_key, dims, split, -0.22, 0.18) * values
    return jnp.clip(values, min=-bound, max=bound).astype(kind)


def setup_inputs(seed: int = 0) -> dict:
    streams_of = jax.random.split(jax.random.key(seed), 5)
    return {
        "row_records": noise(streams_of[0], (NWIN, NR, SAMPLES), 1.0, 6.0, ((0, 4), (1, 8))),
        "row_valid": place_ends((jax.random.randint(streams_of[1], (NWIN, NR), 0, 4) < 3).astype(jnp.int32), jax.random.fold_in(streams_of[1], 1), 0, 1),
        "col_records": noise(streams_of[2], (NWIN, NC, SAMPLES), 1.0, 6.0, ((0, 8), (1, 4))),
        "col_valid": place_ends((jax.random.randint(streams_of[3], (NWIN, NC), 0, 4) < 3).astype(jnp.int32), jax.random.fold_in(streams_of[3], 1), 0, 1),
    }


def reference(row_records, row_valid, col_records, col_valid):
    lag_count = 2 * LAG + 1
    row_masked = row_records * row_valid[:, :, None].astype(jnp.bfloat16)
    col_masked = col_records * col_valid[:, :, None].astype(jnp.bfloat16)
    col_padded = jnp.pad(col_masked, ((0, 0), (0, 0), (LAG, LAG)))
    offsets = jnp.arange(WB, dtype=jnp.int32)

    def one_block(block):
        blocks = (block - jnp.arange(STEPS, dtype=jnp.int32)) % N_COL
        windows = (blocks[:, None] * WB + offsets[None, :]).reshape(-1)
        start = (block * RC).astype(jnp.int32)
        left = lax.dynamic_slice_in_dim(row_masked[windows], start, RC, 1).astype(jnp.float32)
        left_flags = lax.dynamic_slice_in_dim(row_valid[windows], start, RC, 1).astype(jnp.float32)
        right = col_padded[windows]
        right_flags = col_valid[windows].astype(jnp.float32)
        count = jnp.dot(right_flags.T, left_flags, precision=lax.Precision.HIGHEST)

        def one_lag(shift):
            piece = lax.dynamic_slice_in_dim(right, shift, SAMPLES, 2).astype(jnp.float32)
            return jnp.einsum('wbs,was->ba', piece, left, precision=lax.Precision.HIGHEST)
        raw = lax.map(one_lag, jnp.arange(lag_count, dtype=jnp.int32))
        return raw / (jnp.sqrt(jnp.float32(SAMPLES)) * jnp.maximum(count, 1.0))
    blocks_out = lax.map(one_block, jnp.arange(N_COL, dtype=jnp.int32))
    return blocks_out.transpose(1, 2, 0, 3).reshape(lag_count, NC, NR)
```

```python
import functools

import jax
import jax.numpy as jnp
from jax import lax
from jax.experimental import pallas as pl
from jax.experimental.pallas import tpu as pltpu
from jax.sharding import PartitionSpec as P

LAG = 32
STEPS = 4
FINE = 8
MESH = pl.DeviceIdType.MESH


def gather_kernel(
    nrow, ncol, rr, rv, cr, cv, left, left_flag, right, right_flag, flag_r, flag_c,
    send_l, send_lf, recv_l, recv_lf, send_c, send_cf, recv_c, recv_cf, local,
):
    r = lax.axis_index("row")
    c = lax.axis_index("col")
    held = rr.shape[0]
    barrier = pltpu.get_barrier_semaphore()
    for d in range(1, nrow):
        pl.semaphore_signal(barrier, inc=1, device_id={"row": lax.rem(r + d, nrow)}, device_id_type=MESH)
    for d in range(1, STEPS):
        pl.semaphore_signal(barrier, inc=1, device_id={"col": lax.rem(c + ncol - d, ncol)}, device_id_type=MESH)
    for i in range(held):
        flag_r[i] = jnp.broadcast_to(rv[i : i + 1, :].astype(jnp.float32), (16, rv.shape[1])).astype(jnp.bfloat16)
    flag_c[0] = jnp.broadcast_to(cv[0:1, :].astype(jnp.float32), (16, cv.shape[1])).astype(jnp.bfloat16)
    pl.semaphore_wait(barrier, nrow - 1 + STEPS - 1)

    def left_copies(i, d):
        slot = lax.rem(c + ncol - (r * held + i), ncol)
        slot = jnp.minimum(slot, STEPS - 1)
        to = {"row": lax.rem(r + d, nrow)}
        return (
            pltpu.make_async_remote_copy(
                rr.at[i], left.at[slot], send_l.at[i, d - 1], recv_l.at[slot], device_id=to, device_id_type=MESH
            ),
            pltpu.make_async_remote_copy(
                flag_r.at[i], left_flag.at[slot], send_lf.at[i, d - 1], recv_lf.at[slot], device_id=to, device_id_type=MESH
            ),
        )

    def left_own(i):
        slot = lax.rem(c + ncol - (r * held + i), ncol)
        slot = jnp.minimum(slot, STEPS - 1)
        return (
            pltpu.make_async_copy(rr.at[i], left.at[slot], local.at[2 * i]),
            pltpu.make_async_copy(flag_r.at[i], left_flag.at[slot], local.at[2 * i + 1]),
        )

    def right_copies(d):
        to = {"col": lax.rem(c + d, ncol)}
        return (
            pltpu.make_async_remote_copy(
                cr.at[0], right.at[d], send_c.at[d - 1], recv_c.at[d], device_id=to, device_id_type=MESH
            ),
            pltpu.make_async_remote_copy(
                flag_c.at[0], right_flag.at[d], send_cf.at[d - 1], recv_cf.at[d], device_id=to, device_id_type=MESH
            ),
        )

    def used(i):
        return lax.rem(c + ncol - (r * held + i), ncol) < STEPS

    own_right = (
        pltpu.make_async_copy(cr.at[0], right.at[0], local.at[2 * held]),
        pltpu.make_async_copy(flag_c.at[0], right_flag.at[0], local.at[2 * held + 1]),
    )
    for d in range(STEPS - 1, 0, -1):
        for copy in right_copies(d):
            copy.start()
    for i in range(held):
        @pl.when(used(i))
        def _():
            for d in range(nrow - 1, 0, -1):
                for copy in left_copies(i, d):
                    copy.start()
            for copy in left_own(i):
                copy.start()
    for copy in own_right:
        copy.start()

    for copy in own_right:
        copy.wait()
    for i in range(held):
        @pl.when(used(i))
        def _():
            for copy in left_own(i):
                copy.wait()
            for d in range(1, nrow):
                for copy in left_copies(i, d):
                    copy.wait_send()
    for d in range(1, STEPS):
        for copy in right_copies(d):
            copy.wait()
    for s in range(STEPS):
        owner = lax.div(lax.rem(c + ncol - s, ncol), held)

        @pl.when(owner != r)
        def _():
            to = {"row": lax.rem(r + 1, nrow)}
            pltpu.make_async_remote_copy(
                rr.at[0], left.at[s], send_l.at[0, 0], recv_l.at[s], device_id=to, device_id_type=MESH
            ).wait_recv()
            pltpu.make_async_remote_copy(
                flag_r.at[0], left_flag.at[s], send_lf.at[0, 0], recv_lf.at[s], device_id=to, device_id_type=MESH
            ).wait_recv()


def correlate_kernel(left, left_flag, right, right_flag, out, padded, stacked, shifted, weights, scale, result, sem):
    samples = left.shape[2]
    rows = left.shape[1]
    cols = right.shape[1]
    coarse = 2 * LAG // FINE + 1
    main = STEPS * samples
    count = jnp.zeros((cols, rows), jnp.float32)
    for w in range(STEPS):
        across = jnp.broadcast_to(right_flag[w, 0:1, :].astype(jnp.float32), (cols, cols)).T
        row_flag = left_flag[w, 0:1, :].astype(jnp.float32)
        count = count + across * row_flag
        mask = across.astype(jnp.bfloat16)
        padded[:, 0:128] = jnp.zeros((cols, 128), jnp.bfloat16)
        padded[:, 128 + samples :] = jnp.zeros((cols, 128), jnp.bfloat16)
        for j in range(samples // 128):
            padded[:, 128 * (j + 1) : 128 * (j + 2)] = right[w, :, 128 * j : 128 * (j + 1)] * mask
        for h in range(coarse):
            begin = 128 + FINE * h - LAG
            stacked[h * cols : (h + 1) * cols, w * samples : (w + 1) * samples] = padded[:, begin : begin + samples]
            stacked[h * cols : (h + 1) * cols, main + w * FINE : main + (w + 1) * FINE] = padded[
                :, begin + samples : begin + samples + FINE
            ]
        shifted[0:FINE, :] = jnp.zeros((FINE, rows), jnp.float32)
        shifted[FINE + samples :, :] = jnp.zeros((FINE, rows), jnp.float32)
        for j in range(samples // 128):
            block = left[w, :, 128 * j : 128 * (j + 1)].astype(jnp.float32).T * row_flag
            shifted[FINE + 128 * j : FINE + 128 * (j + 1), :] = block
        for g in range(FINE):
            weights[w * samples : (w + 1) * samples, g * rows : (g + 1) * rows] = shifted[
                FINE - g : FINE - g + samples, :
            ].astype(jnp.bfloat16)
            weights[main + w * FINE : main + (w + 1) * FINE, g * rows : (g + 1) * rows] = shifted[
                FINE - g + samples : 2 * FINE - g + samples, :
            ].astype(jnp.bfloat16)
    scale[...] = 1.0 / (jnp.sqrt(jnp.float32(samples)) * jnp.maximum(count, 1.0))

    copies = []
    for p in range(FINE // 2):
        for h in range(coarse):
            single = h == coarse - 1
            if single and p > 0:
                continue
            width = rows if single else 2 * rows
            product = jnp.dot(
                stacked[h * cols : (h + 1) * cols, :],
                weights[:, 2 * p * rows : 2 * p * rows + width],
                preferred_element_type=jnp.float32,
            )
            for q in range(width // rows):
                lag = FINE * h + 2 * p + q
                result[lag] = product[:, q * rows : (q + 1) * rows] * scale[...]
                copy = pltpu.make_async_copy(result.at[lag], out.at[lag], sem.at[lag])
                copy.start()
                copies.append(copy)
    for copy in copies:
        copy.wait()


def shards(row_records, row_valid, col_records, col_valid):
    nrow = lax.axis_size("row")
    ncol = lax.axis_size("col")
    held, rows, samples = row_records.shape
    cols = col_records.shape[1]
    lags = 2 * LAG + 1
    coarse = 2 * LAG // FINE + 1
    any_space = pl.BlockSpec(memory_space=pl.ANY)
    vmem = pl.BlockSpec(memory_space=pltpu.VMEM)
    dma = pltpu.SemaphoreType.DMA
    gathered = pl.pallas_call(
        functools.partial(gather_kernel, nrow, ncol),
        out_shape=(
            jax.ShapeDtypeStruct((STEPS, rows, samples), jnp.bfloat16),
            jax.ShapeDtypeStruct((STEPS, 16, rows), jnp.bfloat16),
            jax.ShapeDtypeStruct((STEPS, cols, samples), jnp.bfloat16),
            jax.ShapeDtypeStruct((STEPS, 16, cols), jnp.bfloat16),
        ),
        in_specs=[any_space, vmem, any_space, vmem],
        out_specs=(any_space,) * 4,
        scratch_shapes=[
            pltpu.VMEM((held, 16, rows), jnp.bfloat16),
            pltpu.VMEM((1, 16, cols), jnp.bfloat16),
            dma((held, nrow - 1)),
            dma((held, nrow - 1)),
            dma((STEPS,)),
            dma((STEPS,)),
            dma((STEPS - 1,)),
            dma((STEPS - 1,)),
            dma((STEPS,)),
            dma((STEPS,)),
            dma((2 * held + 2,)),
        ],
        compiler_params=pltpu.CompilerParams(collective_id=0, has_side_effects=True),
        name="gather",
    )(row_records, row_valid, col_records, col_valid)
    depth = STEPS * (samples + FINE)
    return pl.pallas_call(
        correlate_kernel,
        out_shape=jax.ShapeDtypeStruct((lags, cols, rows), jnp.float32),
        in_specs=[vmem] * 4,
        out_specs=any_space,
        scratch_shapes=[
            pltpu.VMEM((cols, samples + 256), jnp.bfloat16),
            pltpu.VMEM((coarse * cols, depth), jnp.bfloat16),
            pltpu.VMEM((samples + 2 * FINE, rows), jnp.float32),
            pltpu.VMEM((depth, FINE * rows), jnp.bfloat16),
            pltpu.VMEM((cols, rows), jnp.float32),
            pltpu.VMEM((lags, cols, rows), jnp.float32),
            dma((lags,)),
        ],
        compiler_params=pltpu.CompilerParams(vmem_limit_bytes=40 * 1024 * 1024),
        name="correlate",
    )(*gathered)


def solution(mesh):
    return jax.shard_map(
        shards,
        mesh=mesh,
        in_specs=(P("row", "col", None), P("row", "col"), P("col", "row", None), P("col", "row")),
        out_specs=P(None, "row", "col"),
        check_vma=False,
    )
```

```python
import functools

import jax
import jax.numpy as jnp
from jax import lax
from jax.experimental import pallas as pl
from jax.experimental.pallas import tpu as pltpu
from jax.sharding import PartitionSpec as P

LAG = 32
STEPS = 4
FINE = 8
FLAG_ROWS = 16
MESH = pl.DeviceIdType.MESH


def gather_kernel(
    nrow, ncol, rr, rv, cr, cv, stacked, weights, scale,
    rr_here, rv_here, cr_here, cv_here, send_left, send_right, left, right, padded, shifted,
    in_sem, send_l, recv_l, pass_l, send_c, recv_c,
):
    r = lax.axis_index("row")
    c = lax.axis_index("col")
    held, rows, samples = rr.shape
    cols = cr.shape[1]
    tiles = samples // 128
    main = STEPS * samples
    coarse = 2 * LAG // FINE + 1
    even = lax.rem(c, 2) == 0
    other_core = r + 1 - 2 * lax.rem(r, 2)

    loads = [
        pltpu.make_async_copy(source, here, in_sem.at[k])
        for k, (source, here) in enumerate(((rv, rv_here), (cv, cv_here), (cr, cr_here), (rr, rr_here)))
    ]
    for load in loads:
        load.start()
    barrier = pltpu.get_barrier_semaphore()
    for d in range(1, nrow):
        pl.semaphore_signal(barrier, inc=1, device_id={"row": lax.rem(r + d, nrow)}, device_id_type=MESH)
    for d in (1, ncol - 1, ncol - 2):
        pl.semaphore_signal(barrier, inc=1, device_id={"col": lax.rem(c + d, ncol)}, device_id_type=MESH)
    for load in loads:
        load.wait()

    flag = cv_here[0:1, :].astype(jnp.float32)
    mask = jnp.broadcast_to(flag, (cols, cols)).T.astype(jnp.bfloat16)
    for j in range(tiles):
        send_right[128 * j : 128 * (j + 1), :] = cr_here[0, :, 128 * j : 128 * (j + 1)] * mask
    send_right[samples:, :] = jnp.broadcast_to(flag, (FLAG_ROWS, cols)).astype(jnp.bfloat16)
    for i in range(held):
        flag = rv_here[i : i + 1, :].astype(jnp.float32)
        for j in range(tiles):
            block = rr_here[i, :, 128 * j : 128 * (j + 1)].astype(jnp.float32).T * flag
            send_left[i, 128 * j : 128 * (j + 1), :] = block.astype(jnp.bfloat16)
        send_left[i, samples:, :] = jnp.broadcast_to(flag, (FLAG_ROWS, rows)).astype(jnp.bfloat16)
    pl.semaphore_wait(barrier, nrow - 1 + 3)

    def right_copy(source, slot, which, step):
        return pltpu.make_async_remote_copy(
            source, right.at[slot - 1], send_c.at[which], recv_c.at[slot - 1],
            device_id={"col": lax.rem(c + ncol + step, ncol)}, device_id_type=MESH,
        )

    def left_copy(source, slot, sender, to):
        return pltpu.make_async_remote_copy(
            source, left.at[slot], sender, recv_l.at[slot], device_id={"row": to}, device_id_type=MESH
        )

    def slot_of(i):
        return lax.rem(c + ncol - (r * held + i), ncol)

    def own_copies(i):
        slot = jnp.minimum(slot_of(i), STEPS - 1)
        copies = []
        for d in range(1, nrow // 2):
            chip = lax.rem(lax.div(r, 2) + d, nrow // 2)
            copies.append(left_copy(send_left.at[i], slot, send_l.at[i, d], 2 * chip + i % 2))
        copies.append(left_copy(send_left.at[i], slot, send_l.at[i, 0], other_core))
        return copies

    two_on = right_copy(send_right, 2, 0, 2)
    own_on = right_copy(send_right, 1, 1, 1)
    pass_back = right_copy(right.at[1], 1, 1, -1)
    pass_on = right_copy(right.at[1], 3, 2, 1)
    two_on.start()

    @pl.when(even)
    def _():
        own_on.start()

    for i in range(held):
        @pl.when(slot_of(i) < STEPS)
        def _():
            for copy in own_copies(i):
                copy.start()
            left[jnp.minimum(slot_of(i), STEPS - 1)] = send_left[i]

    padded[:, 0:128] = jnp.zeros((cols, 128), jnp.bfloat16)
    padded[:, 128 + samples :] = jnp.zeros((cols, 128), jnp.bfloat16)
    shifted[0:FINE, :] = jnp.zeros((FINE, rows), jnp.float32)
    shifted[FINE + samples :, :] = jnp.zeros((FINE, rows), jnp.float32)

    def stack(w, source):
        for j in range(tiles):
            padded[:, 128 * (j + 1) : 128 * (j + 2)] = source[128 * j : 128 * (j + 1), :]
        for h in range(coarse):
            begin = 128 + FINE * h - LAG
            lines = slice(h * cols, (h + 1) * cols)
            stacked[lines, w * samples : (w + 1) * samples] = padded[:, begin : begin + samples]
            stacked[lines, main + w * FINE : main + (w + 1) * FINE] = padded[:, begin + samples : begin + samples + FINE]

    def weigh(w):
        shifted[FINE : FINE + samples, :] = left[w, 0:samples, :].astype(jnp.float32)
        for g in range(FINE):
            lanes = slice(g * rows, (g + 1) * rows)
            weights[w * samples : (w + 1) * samples, lanes] = shifted[FINE - g : FINE - g + samples, :].astype(jnp.bfloat16)
            weights[main + w * FINE : main + (w + 1) * FINE, lanes] = shifted[
                FINE - g + samples : 2 * FINE - g + samples, :
            ].astype(jnp.bfloat16)

    stack(0, send_right)

    two_on.wait_recv()
    pass_on.start()

    @pl.when(jnp.logical_not(even))
    def _():
        pass_back.start()

    def facts(s):
        window = lax.rem(c + ncol - s, ncol)
        owner = lax.div(window, held)
        passes = jnp.logical_and(
            lax.div(owner, 2) != lax.div(r, 2), lax.rem(lax.rem(window, held), 2) == lax.rem(r, 2)
        )
        return owner, passes

    def pass_copy(s):
        return left_copy(left.at[s], s, pass_l.at[s], other_core)

    for s in range(STEPS):
        owner, passes = facts(s)

        @pl.when(passes)
        def _():
            left_copy(send_left.at[0], s, pass_l.at[s], other_core).wait_recv()
            pass_copy(s).start()

    stack(2, right.at[1])
    for s in range(STEPS):
        owner, passes = facts(s)

        @pl.when(jnp.logical_and(owner != r, jnp.logical_not(passes)))
        def _():
            left_copy(send_left.at[0], s, pass_l.at[s], other_core).wait_recv()

        weigh(s)
    own_on.wait_recv()
    stack(1, right.at[0])
    pass_on.wait_recv()
    stack(3, right.at[2])
    count = jnp.zeros((cols, rows), jnp.float32)
    for s in range(STEPS):
        source = send_right if s == 0 else right.at[s - 1]
        col_flag = source[samples : samples + FLAG_ROWS, :].astype(jnp.float32)[0:1, :]
        row_flag = left[s, samples : samples + FLAG_ROWS, :].astype(jnp.float32)[0:1, :]
        count = count + jnp.broadcast_to(col_flag, (cols, cols)).T * row_flag
    scale[...] = 1.0 / (jnp.sqrt(jnp.float32(samples)) * jnp.maximum(count, 1.0))

    two_on.wait_send()
    own_on.wait_send()
    pass_on.wait_send()
    for i in range(held):
        @pl.when(slot_of(i) < STEPS)
        def _():
            for copy in own_copies(i):
                copy.wait_send()
    for s in range(STEPS):
        owner, passes = facts(s)

        @pl.when(passes)
        def _():
            pass_copy(s).wait_send()


def correlate_kernel(stacked, weights, scale, out, result, sem):
    cols, rows = scale.shape
    coarse = stacked.shape[0] // cols
    copies = []
    for p in range(FINE // 2):
        for h in range(coarse):
            single = h == coarse - 1
            if single and p > 0:
                continue
            width = rows if single else 2 * rows
            product = jnp.dot(
                stacked[h * cols : (h + 1) * cols, :],
                weights[:, 2 * p * rows : 2 * p * rows + width],
                preferred_element_type=jnp.float32,
            )
            for q in range(width // rows):
                lag = FINE * h + 2 * p + q
                result[lag] = product[:, q * rows : (q + 1) * rows] * scale[...]
                copy = pltpu.make_async_copy(result.at[lag], out.at[lag], sem.at[lag])
                copy.start()
                copies.append(copy)
    for copy in copies:
        copy.wait()


def shards(row_records, row_valid, col_records, col_valid):
    nrow = lax.axis_size("row")
    ncol = lax.axis_size("col")
    held, rows, samples = row_records.shape
    cols = col_records.shape[1]
    lags = 2 * LAG + 1
    coarse = 2 * LAG // FINE + 1
    depth = STEPS * (samples + FINE)
    any_space = pl.BlockSpec(memory_space=pl.ANY)
    vmem = pl.BlockSpec(memory_space=pltpu.VMEM)
    dma = pltpu.SemaphoreType.DMA
    operands = pl.pallas_call(
        functools.partial(gather_kernel, nrow, ncol),
        out_shape=(
            jax.ShapeDtypeStruct((coarse * cols, depth), jnp.bfloat16),
            jax.ShapeDtypeStruct((depth, FINE * rows), jnp.bfloat16),
            jax.ShapeDtypeStruct((cols, rows), jnp.float32),
        ),
        in_specs=[pl.BlockSpec(memory_space=pltpu.HBM)] * 4,
        out_specs=(vmem,) * 3,
        scratch_shapes=[
            pltpu.VMEM((held, rows, samples), jnp.bfloat16),
            pltpu.VMEM((held, rows), jnp.int32),
            pltpu.VMEM((1, cols, samples), jnp.bfloat16),
            pltpu.VMEM((1, cols), jnp.int32),
            pltpu.VMEM((held, samples + FLAG_ROWS, rows), jnp.bfloat16),
            pltpu.VMEM((samples + FLAG_ROWS, cols), jnp.bfloat16),
            pltpu.VMEM((STEPS, samples + FLAG_ROWS, rows), jnp.bfloat16),
            pltpu.VMEM((STEPS - 1, samples + FLAG_ROWS, cols), jnp.bfloat16),
            pltpu.VMEM((cols, samples + 256), jnp.bfloat16),
            pltpu.VMEM((samples + 2 * FINE, rows), jnp.float32),
            dma((4,)),
            dma((held, nrow // 2)),
            dma((STEPS,)),
            dma((STEPS,)),
            dma((STEPS - 1,)),
            dma((STEPS - 1,)),
        ],
        compiler_params=pltpu.CompilerParams(
            collective_id=0, has_side_effects=True, vmem_limit_bytes=14 * 1024 * 1024
        ),
        name="gather",
    )(row_records, row_valid, col_records, col_valid)
    return pl.pallas_call(
        correlate_kernel,
        out_shape=jax.ShapeDtypeStruct((lags, cols, rows), jnp.float32),
        in_specs=[vmem] * 3,
        out_specs=any_space,
        scratch_shapes=[pltpu.VMEM((lags, cols, rows), jnp.float32), dma((lags,))],
        compiler_params=pltpu.CompilerParams(vmem_limit_bytes=16 * 1024 * 1024),
        name="correlate",
    )(*operands)


def solution(mesh):
    return jax.shard_map(
        shards,
        mesh=mesh,
        in_specs=(P("row", "col", None), P("row", "col"), P("col", "row", None), P("col", "row")),
        out_specs=P(None, "row", "col"),
        check_vma=False,
    )
```

```python
import functools

import jax
import jax.numpy as jnp
from jax import lax
from jax.experimental import pallas as pl
from jax.experimental.pallas import tpu as pltpu
from jax.sharding import PartitionSpec as P

LAG = 32
STEPS = 4
FINE = 8
FLAG_ROWS = 16
MESH = pl.DeviceIdType.MESH


def gather_kernel(
    nrow, ncol, rr, rv, cr, cv, stacked, weights, partial, scale,
    stacked_a, weights_a,    rr_here, rv_here, cr_here, cv_here, send_left, send_right, left, right, padded, shifted,
    in_sem, send_l, recv_l, pass_l, send_c, recv_c,
):
    r = lax.axis_index("row")
    c = lax.axis_index("col")
    held, rows, samples = rr.shape
    cols = cr.shape[1]
    tiles = samples // 128
    coarse = 2 * LAG // FINE + 1
    even = lax.rem(c, 2) == 0
    neighbour = ncol + 1 - 2 * lax.rem(c, 2)
    other_core = r + 1 - 2 * lax.rem(r, 2)

    loads = [
        pltpu.make_async_copy(source, here, in_sem.at[k])
        for k, (source, here) in enumerate(((rv, rv_here), (cv, cv_here), (cr, cr_here), (rr, rr_here)))
    ]
    for load in loads:
        load.start()
    barrier = pltpu.get_barrier_semaphore()
    for d in range(1, nrow):
        pl.semaphore_signal(barrier, inc=1, device_id={"row": lax.rem(r + d, nrow)}, device_id_type=MESH)
    for d in (ncol - 2, neighbour):
        pl.semaphore_signal(barrier, inc=1, device_id={"col": lax.rem(c + d, ncol)}, device_id_type=MESH)

    @pl.when(even)
    def _():
        pl.semaphore_signal(barrier, inc=1, device_id={"col": lax.rem(c + ncol - 3, ncol)}, device_id_type=MESH)

    for load in loads:
        load.wait()

    flag = cv_here[0:1, :].astype(jnp.float32)
    mask = jnp.broadcast_to(flag, (cols, cols)).T.astype(jnp.bfloat16)
    for j in range(tiles):
        send_right[128 * j : 128 * (j + 1), :] = cr_here[0, :, 128 * j : 128 * (j + 1)] * mask
    send_right[samples:, :] = jnp.broadcast_to(flag, (FLAG_ROWS, cols)).astype(jnp.bfloat16)
    for i in range(held):
        flag = rv_here[i : i + 1, :].astype(jnp.float32)
        for j in range(tiles):
            block = rr_here[i, :, 128 * j : 128 * (j + 1)].astype(jnp.float32).T * flag
            send_left[i, 128 * j : 128 * (j + 1), :] = block.astype(jnp.bfloat16)
        send_left[i, samples:, :] = jnp.broadcast_to(flag, (FLAG_ROWS, rows)).astype(jnp.bfloat16)
    pl.semaphore_wait(barrier, nrow - 1 + 2 + lax.rem(c, 2))

    pieces = [slice(128 * j, 128 * (j + 1)) for j in range(tiles - 1)] + [slice(128 * (tiles - 1), samples + FLAG_ROWS)]

    def right_copy(source, slot, which, step):
        return [
            pltpu.make_async_remote_copy(
                source.at[lines], right.at[slot - 1, lines], send_c.at[which, k], recv_c.at[slot - 1, k],
                device_id={"col": lax.rem(c + ncol + step, ncol)}, device_id_type=MESH,
            )
            for k, lines in enumerate(pieces)
        ]

    def left_copy(source, slot, sender, to):
        return pltpu.make_async_remote_copy(
            source, left.at[slot], sender, recv_l.at[slot], device_id={"row": to}, device_id_type=MESH
        )

    def slot_of(i):
        return lax.rem(c + ncol - (r * held + i), ncol)

    def own_copies(i):
        slot = jnp.minimum(slot_of(i), STEPS - 1)
        copies = []
        for d in range(1, nrow // 2):
            chip = lax.rem(lax.div(r, 2) + d, nrow // 2)
            copies.append(left_copy(send_left.at[i], slot, send_l.at[i, d], 2 * chip + i % 2))
        copies.append(left_copy(send_left.at[i], slot, send_l.at[i, 0], other_core))
        return copies

    two_on = right_copy(send_right, 2, 0, 2)
    own_on = right_copy(send_right, 1, 1, 1)
    pass_back = right_copy(right.at[1], 1, 1, -1)
    pass_on = right_copy(right.at[1], 3, 2, 1)
    three_on = right_copy(send_right, 3, 2, 3)
    for piece in two_on:
        piece.start()

    @pl.when(jnp.logical_not(even))
    def _():
        for piece in three_on:
            piece.start()

    @pl.when(even)
    def _():
        for piece in own_on:
            piece.start()

    for i in range(held):
        @pl.when(slot_of(i) < STEPS)
        def _():
            for copy in own_copies(i):
                copy.start()
            left[jnp.minimum(slot_of(i), STEPS - 1)] = send_left[i]

    padded[:, 0:128] = jnp.zeros((cols, 128), jnp.bfloat16)
    padded[:, 128 + samples :] = jnp.zeros((cols, 128), jnp.bfloat16)
    shifted[0:FINE, :] = jnp.zeros((FINE, rows), jnp.float32)
    shifted[FINE + samples :, :] = jnp.zeros((FINE, rows), jnp.float32)

    def stack(p, source):
        target, begin_at = (stacked_a, p * samples) if p < STEPS - 1 else (stacked, 0)
        for j in range(tiles):
            padded[:, 128 * (j + 1) : 128 * (j + 2)] = source[128 * j : 128 * (j + 1), :]
        for h in range(coarse):
            begin = 128 + FINE * h - LAG
            lines = slice(h * cols, (h + 1) * cols)
            target[lines, begin_at : begin_at + samples] = padded[:, begin : begin + samples]
            stacked[lines, samples + p * FINE : samples + (p + 1) * FINE] = padded[:, begin + samples : begin + samples + FINE]

    def weigh(p, slot):
        target, begin_at = (weights_a, p * samples) if p < STEPS - 1 else (weights, 0)
        shifted[FINE : FINE + samples, :] = left[slot, 0:samples, :].astype(jnp.float32)
        for g in range(FINE):
            lanes = slice(g * rows, (g + 1) * rows)
            target[begin_at : begin_at + samples, lanes] = shifted[FINE - g : FINE - g + samples, :].astype(jnp.bfloat16)
            weights[samples + p * FINE : samples + (p + 1) * FINE, lanes] = shifted[
                FINE - g + samples : 2 * FINE - g + samples, :
            ].astype(jnp.bfloat16)

    def facts(s):
        window = lax.rem(c + ncol - s, ncol)
        owner = lax.div(window, held)
        passes = jnp.logical_and(
            lax.div(owner, 2) != lax.div(r, 2), lax.rem(lax.rem(window, held), 2) == lax.rem(r, 2)
        )
        return owner, passes

    def pass_copy(s):
        return left_copy(left.at[s], s, pass_l.at[s], other_core)

    def left_wait(s):
        owner, passes = facts(s)

        @pl.when(jnp.logical_and(owner != r, jnp.logical_not(passes)))
        def _():
            left_copy(send_left.at[0], s, pass_l.at[0], other_core).wait_recv()

    def right_wait(slot):
        for piece in right_copy(send_right, slot, 0, 2):
            piece.wait_recv()

    def multiply(first, last, add):
        for p in range(FINE // 2):
            for h in range(coarse):
                single = h == coarse - 1
                if single and p > 0:
                    continue
                width = rows if single else 2 * rows
                product = jnp.dot(
                    stacked_a[h * cols : (h + 1) * cols, first:last],
                    weights_a[first:last, 2 * p * rows : 2 * p * rows + width],
                    preferred_element_type=jnp.float32,
                )
                for q in range(width // rows):
                    lag = FINE * h + 2 * p + q
                    term = product[:, q * rows : (q + 1) * rows]
                    partial[lag] = partial[lag] + term if add else term

    stack(0, send_right)

    for k in range(tiles):
        two_on[k].wait_recv()

        @pl.when(even)
        def _():
            pass_on[k].start()

        @pl.when(jnp.logical_not(even))
        def _():
            pass_back[k].start()

    for s in range(STEPS):
        owner, passes = facts(s)

        @pl.when(passes)
        def _():
            left_copy(send_left.at[0], s, pass_l.at[s], other_core).wait_recv()
            pass_copy(s).start()

    stack(1, right.at[1])
    for p, slot in ((0, 0), (1, 2)):
        left_wait(slot)
        weigh(p, slot)
    multiply(0, 2 * samples, False)
    third = 1 + 2 * lax.rem(c + 1, 2)
    fourth = 4 - third
    right_wait(third)
    stack(2, right.at[third - 1])
    left_wait(third)
    weigh(2, third)
    multiply(2 * samples, 3 * samples, True)
    right_wait(fourth)
    stack(3, right.at[fourth - 1])
    left_wait(fourth)
    weigh(3, fourth)
    count = jnp.zeros((cols, rows), jnp.float32)
    for s in range(STEPS):
        source = send_right if s == 0 else right.at[s - 1]
        col_flag = source[samples : samples + FLAG_ROWS, :].astype(jnp.float32)[0:1, :]
        row_flag = left[s, samples : samples + FLAG_ROWS, :].astype(jnp.float32)[0:1, :]
        count = count + jnp.broadcast_to(col_flag, (cols, cols)).T * row_flag
    scale[...] = 1.0 / (jnp.sqrt(jnp.float32(samples)) * jnp.maximum(count, 1.0))

    for piece in two_on + own_on + pass_on:
        piece.wait_send()
    for i in range(held):
        @pl.when(slot_of(i) < STEPS)
        def _():
            for copy in own_copies(i):
                copy.wait_send()
    for s in range(STEPS):
        owner, passes = facts(s)

        @pl.when(passes)
        def _():
            pass_copy(s).wait_send()


def correlate_kernel(stacked, weights, partial, scale, out, result, sem):
    cols, rows = scale.shape
    coarse = stacked.shape[0] // cols
    copies = []
    for p in range(FINE // 2):
        for h in range(coarse):
            single = h == coarse - 1
            if single and p > 0:
                continue
            width = rows if single else 2 * rows
            product = jnp.dot(
                stacked[h * cols : (h + 1) * cols, :],
                weights[:, 2 * p * rows : 2 * p * rows + width],
                preferred_element_type=jnp.float32,
            )
            for q in range(width // rows):
                lag = FINE * h + 2 * p + q
                result[lag] = (partial[lag] + product[:, q * rows : (q + 1) * rows]) * scale[...]
                copy = pltpu.make_async_copy(result.at[lag], out.at[lag], sem.at[lag])
                copy.start()
                copies.append(copy)
    for copy in copies:
        copy.wait()


def shards(row_records, row_valid, col_records, col_valid):
    nrow = lax.axis_size("row")
    ncol = lax.axis_size("col")
    held, rows, samples = row_records.shape
    cols = col_records.shape[1]
    lags = 2 * LAG + 1
    coarse = 2 * LAG // FINE + 1
    early = (STEPS - 1) * samples
    late = samples + STEPS * FINE
    any_space = pl.BlockSpec(memory_space=pl.ANY)
    vmem = pl.BlockSpec(memory_space=pltpu.VMEM)
    dma = pltpu.SemaphoreType.DMA
    operands = pl.pallas_call(
        functools.partial(gather_kernel, nrow, ncol),
        out_shape=(
            jax.ShapeDtypeStruct((coarse * cols, late), jnp.bfloat16),
            jax.ShapeDtypeStruct((late, FINE * rows), jnp.bfloat16),
            jax.ShapeDtypeStruct((lags, cols, rows), jnp.float32),
            jax.ShapeDtypeStruct((cols, rows), jnp.float32),
        ),
        in_specs=[pl.BlockSpec(memory_space=pltpu.HBM)] * 4,
        out_specs=(vmem,) * 4,
        scratch_shapes=[
            pltpu.VMEM((coarse * cols, early), jnp.bfloat16),
            pltpu.VMEM((early, FINE * rows), jnp.bfloat16),
            pltpu.VMEM((held, rows, samples), jnp.bfloat16),
            pltpu.VMEM((held, rows), jnp.int32),
            pltpu.VMEM((1, cols, samples), jnp.bfloat16),
            pltpu.VMEM((1, cols), jnp.int32),
            pltpu.VMEM((held, samples + FLAG_ROWS, rows), jnp.bfloat16),
            pltpu.VMEM((samples + FLAG_ROWS, cols), jnp.bfloat16),
            pltpu.VMEM((STEPS, samples + FLAG_ROWS, rows), jnp.bfloat16),
            pltpu.VMEM((STEPS - 1, samples + FLAG_ROWS, cols), jnp.bfloat16),
            pltpu.VMEM((cols, samples + 256), jnp.bfloat16),
            pltpu.VMEM((samples + 2 * FINE, rows), jnp.float32),
            dma((4,)),
            dma((held, nrow // 2)),
            dma((STEPS,)),
            dma((STEPS,)),
            dma((STEPS - 1, samples // 128)),
            dma((STEPS - 1, samples // 128)),
        ],
        compiler_params=pltpu.CompilerParams(
            collective_id=0, has_side_effects=True, vmem_limit_bytes=20 * 1024 * 1024
        ),
        name="gather",
    )(*(pltpu.with_memory_space_constraint(x, pltpu.HBM) for x in (row_records, row_valid, col_records, col_valid)))
    return pl.pallas_call(
        correlate_kernel,
        out_shape=jax.ShapeDtypeStruct((lags, cols, rows), jnp.float32),
        in_specs=[vmem] * 4,
        out_specs=any_space,
        scratch_shapes=[pltpu.VMEM((lags, cols, rows), jnp.float32), dma((lags,))],
        compiler_params=pltpu.CompilerParams(vmem_limit_bytes=16 * 1024 * 1024),
        name="correlate",
    )(*operands)


def solution(mesh):
    return jax.shard_map(
        shards,
        mesh=mesh,
        in_specs=(P("row", "col", None), P("row", "col"), P("col", "row", None), P("col", "row")),
        out_specs=P(None, "row", "col"),
        check_vma=False,
    )
```

```python
import functools

import jax
import jax.numpy as jnp
from jax import lax
from jax.experimental import pallas as pl
from jax.experimental.pallas import tpu as pltpu
from jax.sharding import PartitionSpec as P

LAG = 32
STEPS = 4
FINE = 8
FLAG_ROWS = 16
MESH = pl.DeviceIdType.MESH


def gather_kernel(
    nrow, ncol, rr, rv, cr, cv, stacked, weights, partial, scale,
    stacked_a, weights_a,    rr_here, rv_here, cr_here, cv_here, send_left, send_right, left, right, padded, shifted,
    in_sem, send_l, recv_l, pass_l, send_c, recv_c, send_relay, recv_relay, relay,
):
    r = lax.axis_index("row")
    c = lax.axis_index("col")
    held, rows, samples = rr.shape
    cols = cr.shape[1]
    tiles = samples // 128
    coarse = 2 * LAG // FINE + 1
    even = lax.rem(c, 2) == 0
    neighbour = ncol + 1 - 2 * lax.rem(c, 2)
    other_core = r + 1 - 2 * lax.rem(r, 2)

    loads = [
        pltpu.make_async_copy(source, here, in_sem.at[k])
        for k, (source, here) in enumerate(((cv, cv_here), (cr, cr_here), (rv, rv_here), (rr, rr_here)))
    ]
    for load in loads:
        load.start()
    barrier = pltpu.get_barrier_semaphore()
    for d in range(1, nrow):
        pl.semaphore_signal(barrier, inc=1, device_id={"row": lax.rem(r + d, nrow)}, device_id_type=MESH)
    for d in (ncol - 2, ncol - 4, neighbour):
        pl.semaphore_signal(barrier, inc=1, device_id={"col": lax.rem(c + d, ncol)}, device_id_type=MESH)

    loads[0].wait()
    loads[1].wait()

    flag = cv_here[0:1, :].astype(jnp.float32)
    mask = jnp.broadcast_to(flag, (cols, cols)).T.astype(jnp.bfloat16)
    for j in range(tiles):
        send_right[128 * j : 128 * (j + 1), :] = cr_here[0, :, 128 * j : 128 * (j + 1)] * mask
    send_right[samples:, :] = jnp.broadcast_to(flag, (FLAG_ROWS, cols)).astype(jnp.bfloat16)
    pl.semaphore_wait(barrier, nrow - 1 + 3)

    pieces = [slice(128 * j, 128 * (j + 1)) for j in range(tiles - 1)] + [slice(128 * (tiles - 1), samples + FLAG_ROWS)]

    def right_copy(source, slot, which, step):
        return [
            pltpu.make_async_remote_copy(
                source.at[lines], right.at[slot - 1, lines], send_c.at[which, k], recv_c.at[slot - 1, k],
                device_id={"col": lax.rem(c + ncol + step, ncol)}, device_id_type=MESH,
            )
            for k, lines in enumerate(pieces)
        ]

    def left_copy(source, slot, sender, to):
        return pltpu.make_async_remote_copy(
            source, left.at[slot], sender, recv_l.at[slot], device_id={"row": to}, device_id_type=MESH
        )

    def slot_of(i):
        return lax.rem(c + ncol - (r * held + i), ncol)

    def own_copies(i):
        slot = jnp.minimum(slot_of(i), STEPS - 1)
        copies = []
        for d in range(1, nrow // 2):
            chip = lax.rem(lax.div(r, 2) + d, nrow // 2)
            copies.append(left_copy(send_left.at[i], slot, send_l.at[i, d], 2 * chip + lax.rem(i, 2)))
        copies.append(left_copy(send_left.at[i], slot, send_l.at[i, 0], other_core))
        return copies

    two_on = right_copy(send_right, 2, 0, 2)
    own_on = right_copy(send_right, 1, 1, 1)
    pass_back = right_copy(right.at[1], 1, 1, -1)
    pass_on = right_copy(right.at[1], 3, 2, 1)

    cut = FLAG_ROWS * -(-(samples + FLAG_ROWS) // (2 * FLAG_ROWS))
    upper, lower, lower_here = slice(0, cut), slice(cut, samples + FLAG_ROWS), slice(0, samples + FLAG_ROWS - cut)

    def relay_copy(source, target, sender, receiver, step):
        return pltpu.make_async_remote_copy(
            source, target, send_relay.at[sender], receiver,
            device_id={"col": lax.rem(c + ncol + step, ncol)}, device_id_type=MESH,
        )

    upper_out = relay_copy(send_right.at[upper], relay.at[upper], 0, recv_relay.at[0], -1)
    lower_out = relay_copy(send_right.at[lower], relay.at[lower_here], 1, recv_relay.at[0], 4)
    upper_on = relay_copy(relay.at[upper], right.at[2, upper], 0, recv_c.at[2, 0], 4)
    lower_on = relay_copy(relay.at[lower_here], right.at[2, lower], 2, recv_c.at[2, 1], -1)
    for piece in two_on:
        piece.start()

    @pl.when(jnp.logical_not(even))
    def _():
        upper_out.start()
        lower_out.start()

    @pl.when(even)
    def _():
        for piece in own_on:
            piece.start()

    loads[2].wait()
    loads[3].wait()
    for i in range(held):
        flag = rv_here[i : i + 1, :].astype(jnp.float32)
        for j in range(tiles):
            block = rr_here[i, :, 128 * j : 128 * (j + 1)].astype(jnp.float32).T * flag
            send_left[i, 128 * j : 128 * (j + 1), :] = block.astype(jnp.bfloat16)
        send_left[i, samples:, :] = jnp.broadcast_to(flag, (FLAG_ROWS, rows)).astype(jnp.bfloat16)
    for k in range(held):
        i = lax.rem(c + k, held)

        @pl.when(slot_of(i) < STEPS)
        def _():
            for copy in own_copies(i):
                copy.start()
            left[jnp.minimum(slot_of(i), STEPS - 1)] = send_left[i]

    padded[:, 0:128] = jnp.zeros((cols, 128), jnp.bfloat16)
    padded[:, 128 + samples :] = jnp.zeros((cols, 128), jnp.bfloat16)
    shifted[0:FINE, :] = jnp.zeros((FINE, rows), jnp.float32)
    shifted[FINE + samples :, :] = jnp.zeros((FINE, rows), jnp.float32)

    def stack(p, source):
        target, begin_at = (stacked_a, p * samples) if p < STEPS - 1 else (stacked, 0)
        for j in range(tiles):
            padded[:, 128 * (j + 1) : 128 * (j + 2)] = source[128 * j : 128 * (j + 1), :]
        for h in range(coarse):
            begin = 128 + FINE * h - LAG
            lines = slice(h * cols, (h + 1) * cols)
            target[lines, begin_at : begin_at + samples] = padded[:, begin : begin + samples]
            stacked[lines, samples + p * FINE : samples + (p + 1) * FINE] = padded[:, begin + samples : begin + samples + FINE]

    def weigh(p, slot):
        target, begin_at = (weights_a, p * samples) if p < STEPS - 1 else (weights, 0)
        shifted[FINE : FINE + samples, :] = left[slot, 0:samples, :].astype(jnp.float32)
        for g in range(FINE):
            lanes = slice(g * rows, (g + 1) * rows)
            target[begin_at : begin_at + samples, lanes] = shifted[FINE - g : FINE - g + samples, :].astype(jnp.bfloat16)
            weights[samples + p * FINE : samples + (p + 1) * FINE, lanes] = shifted[
                FINE - g + samples : 2 * FINE - g + samples, :
            ].astype(jnp.bfloat16)

    def facts(s):
        window = lax.rem(c + ncol - s, ncol)
        owner = lax.div(window, held)
        passes = jnp.logical_and(
            lax.div(owner, 2) != lax.div(r, 2), lax.rem(lax.rem(window, held), 2) == lax.rem(r, 2)
        )
        return owner, passes

    def pass_copy(s):
        return left_copy(left.at[s], s, pass_l.at[s], other_core)

    def left_wait(s):
        owner, passes = facts(s)

        @pl.when(jnp.logical_and(owner != r, jnp.logical_not(passes)))
        def _():
            left_copy(send_left.at[0], s, pass_l.at[0], other_core).wait_recv()

    def right_wait(slot):
        for piece in right_copy(send_right, slot, 0, 2):
            piece.wait_recv()

    def multiply(first, last, add):
        for p in range(FINE // 2):
            for h in range(coarse):
                single = h == coarse - 1
                if single and p > 0:
                    continue
                width = rows if single else 2 * rows
                product = jnp.dot(
                    stacked_a[h * cols : (h + 1) * cols, first:last],
                    weights_a[first:last, 2 * p * rows : 2 * p * rows + width],
                    preferred_element_type=jnp.float32,
                )
                for q in range(width // rows):
                    lag = FINE * h + 2 * p + q
                    term = product[:, q * rows : (q + 1) * rows]
                    partial[lag] = partial[lag] + term if add else term

    def left_pass(s):
        owner, passes = facts(s)

        @pl.when(passes)
        def _():
            left_copy(send_left.at[0], s, pass_l.at[s], other_core).wait_recv()
            pass_copy(s).start()

    @pl.when(even)
    def _():
        upper_out.wait_recv()
        upper_on.start()

    stack(0, send_right)
    left_pass(0)
    left_wait(0)
    weigh(0, 0)
    multiply(0, samples, False)

    for k in range(tiles):
        two_on[k].wait_recv()

        @pl.when(even)
        def _():
            pass_on[k].start()

        @pl.when(jnp.logical_not(even))
        def _():
            pass_back[k].start()

    @pl.when(jnp.logical_not(even))
    def _():
        lower_out.wait_recv()
        lower_on.start()

    for s in (2, 1, 3):
        left_pass(s)
    stack(1, right.at[1])
    left_wait(2)
    weigh(1, 2)
    multiply(samples, 2 * samples, True)
    left_wait(1)
    weigh(2, 1)
    right_wait(1)
    stack(2, right.at[0])
    multiply(2 * samples, 3 * samples, True)
    left_wait(3)
    weigh(3, 3)
    @pl.when(even)
    def _():
        upper_on.wait_recv()
        lower_on.wait_recv()

    @pl.when(jnp.logical_not(even))
    def _():
        right_wait(3)

    stack(3, right.at[2])
    count = jnp.zeros((cols, rows), jnp.float32)
    for s in range(STEPS):
        source = send_right if s == 0 else right.at[s - 1]
        col_flag = source[samples : samples + FLAG_ROWS, :].astype(jnp.float32)[0:1, :]
        row_flag = left[s, samples : samples + FLAG_ROWS, :].astype(jnp.float32)[0:1, :]
        count = count + jnp.broadcast_to(col_flag, (cols, cols)).T * row_flag
    scale[...] = 1.0 / (jnp.sqrt(jnp.float32(samples)) * jnp.maximum(count, 1.0))

    for piece in two_on + own_on:
        piece.wait_send()
    upper_out.wait_send()

    @pl.when(even)
    def _():
        for piece in pass_on:
            piece.wait_send()

    @pl.when(jnp.logical_not(even))
    def _():
        lower_out.wait_send()
        lower_on.wait_send()

    for i in range(held):
        @pl.when(slot_of(i) < STEPS)
        def _():
            for copy in own_copies(i):
                copy.wait_send()
    for s in range(STEPS):
        owner, passes = facts(s)

        @pl.when(passes)
        def _():
            pass_copy(s).wait_send()


def correlate_kernel(stacked, weights, partial, scale, out, result, sem):
    cols, rows = scale.shape
    coarse = stacked.shape[0] // cols
    copies = []
    for p in range(FINE // 2):
        for h in range(coarse):
            single = h == coarse - 1
            if single and p > 0:
                continue
            width = rows if single else 2 * rows
            product = jnp.dot(
                stacked[h * cols : (h + 1) * cols, :],
                weights[:, 2 * p * rows : 2 * p * rows + width],
                preferred_element_type=jnp.float32,
            )
            for q in range(width // rows):
                lag = FINE * h + 2 * p + q
                result[lag] = (partial[lag] + product[:, q * rows : (q + 1) * rows]) * scale[...]
                copy = pltpu.make_async_copy(result.at[lag], out.at[lag], sem.at[lag])
                copy.start()
                copies.append(copy)
    for copy in copies:
        copy.wait()


def shards(row_records, row_valid, col_records, col_valid):
    nrow = lax.axis_size("row")
    ncol = lax.axis_size("col")
    held, rows, samples = row_records.shape
    cols = col_records.shape[1]
    lags = 2 * LAG + 1
    coarse = 2 * LAG // FINE + 1
    early = (STEPS - 1) * samples
    late = samples + STEPS * FINE
    any_space = pl.BlockSpec(memory_space=pl.ANY)
    vmem = pl.BlockSpec(memory_space=pltpu.VMEM)
    dma = pltpu.SemaphoreType.DMA
    operands = pl.pallas_call(
        functools.partial(gather_kernel, nrow, ncol),
        out_shape=(
            jax.ShapeDtypeStruct((coarse * cols, late), jnp.bfloat16),
            jax.ShapeDtypeStruct((late, FINE * rows), jnp.bfloat16),
            jax.ShapeDtypeStruct((lags, cols, rows), jnp.float32),
            jax.ShapeDtypeStruct((cols, rows), jnp.float32),
        ),
        in_specs=[pl.BlockSpec(memory_space=pltpu.HBM)] * 4,
        out_specs=(vmem,) * 4,
        scratch_shapes=[
            pltpu.VMEM((coarse * cols, early), jnp.bfloat16),
            pltpu.VMEM((early, FINE * rows), jnp.bfloat16),
            pltpu.VMEM((held, rows, samples), jnp.bfloat16),
            pltpu.VMEM((held, rows), jnp.int32),
            pltpu.VMEM((1, cols, samples), jnp.bfloat16),
            pltpu.VMEM((1, cols), jnp.int32),
            pltpu.VMEM((held, samples + FLAG_ROWS, rows), jnp.bfloat16),
            pltpu.VMEM((samples + FLAG_ROWS, cols), jnp.bfloat16),
            pltpu.VMEM((STEPS, samples + FLAG_ROWS, rows), jnp.bfloat16),
            pltpu.VMEM((STEPS - 1, samples + FLAG_ROWS, cols), jnp.bfloat16),
            pltpu.VMEM((cols, samples + 256), jnp.bfloat16),
            pltpu.VMEM((samples + 2 * FINE, rows), jnp.float32),
            dma((4,)),
            dma((held, nrow // 2)),
            dma((STEPS,)),
            dma((STEPS,)),
            dma((STEPS - 1, samples // 128)),
            dma((STEPS - 1, samples // 128)),
            dma((3,)),
            dma((1,)),
            pltpu.VMEM((samples + FLAG_ROWS, cols), jnp.bfloat16),
        ],
        compiler_params=pltpu.CompilerParams(
            collective_id=0, has_side_effects=True, vmem_limit_bytes=20 * 1024 * 1024
        ),
        name="gather",
    )(*(pltpu.with_memory_space_constraint(x, pltpu.HBM) for x in (row_records, row_valid, col_records, col_valid)))
    return pl.pallas_call(
        correlate_kernel,
        out_shape=jax.ShapeDtypeStruct((lags, cols, rows), jnp.float32),
        in_specs=[vmem] * 4,
        out_specs=any_space,
        scratch_shapes=[pltpu.VMEM((lags, cols, rows), jnp.float32), dma((lags,))],
        compiler_params=pltpu.CompilerParams(vmem_limit_bytes=16 * 1024 * 1024),
        name="correlate",
    )(*operands)


def solution(mesh):
    return jax.shard_map(
        shards,
        mesh=mesh,
        in_specs=(P("row", "col", None), P("row", "col"), P("col", "row", None), P("col", "row")),
        out_specs=P(None, "row", "col"),
        check_vma=False,
    )
```

```python
import functools

import jax
import jax.numpy as jnp
from jax import lax
from jax.experimental import pallas as pl
from jax.experimental.pallas import tpu as pltpu
from jax.sharding import PartitionSpec as P

LAG = 32
STEPS = 4
FINE = 8
FLAG_ROWS = 16
MESH = pl.DeviceIdType.MESH


def gather_kernel(
    nrow, ncol, rr, rv, cr, cv, stacked, weights, partial, scale,
    stacked_a, weights_a,    rr_here, rv_here, cr_here, cv_here, send_left, send_right, left, right, padded, shifted,
    in_sem, send_l, recv_l, pass_l, send_c, recv_c, send_relay, recv_relay, relay,
):
    r = lax.axis_index("row")
    c = lax.axis_index("col")
    held, rows, samples = rr.shape
    cols = cr.shape[1]
    tiles = samples // 128
    coarse = 2 * LAG // FINE + 1
    even = lax.rem(c, 2) == 0
    neighbour = ncol + 1 - 2 * lax.rem(c, 2)
    other_core = r + 1 - 2 * lax.rem(r, 2)

    loads = [
        pltpu.make_async_copy(source, here, in_sem.at[k])
        for k, (source, here) in enumerate(((cv, cv_here), (cr, cr_here), (rv, rv_here), (rr, rr_here)))
    ]
    for load in loads:
        load.start()
    barrier = pltpu.get_barrier_semaphore()
    for d in range(1, nrow):
        pl.semaphore_signal(barrier, inc=1, device_id={"row": lax.rem(r + d, nrow)}, device_id_type=MESH)
    for d in (ncol - 2, ncol - 4, neighbour):
        pl.semaphore_signal(barrier, inc=1, device_id={"col": lax.rem(c + d, ncol)}, device_id_type=MESH)

    loads[0].wait()
    loads[1].wait()

    flag = cv_here[0:1, :].astype(jnp.float32)
    mask = jnp.broadcast_to(flag, (cols, cols)).T.astype(jnp.bfloat16)
    for j in range(tiles):
        send_right[128 * j : 128 * (j + 1), :] = cr_here[0, :, 128 * j : 128 * (j + 1)] * mask
    send_right[samples:, :] = jnp.broadcast_to(flag, (FLAG_ROWS, cols)).astype(jnp.bfloat16)
    pl.semaphore_wait(barrier, nrow - 1 + 3)

    pieces = [slice(128 * j, 128 * (j + 1)) for j in range(tiles - 1)] + [slice(128 * (tiles - 1), samples + FLAG_ROWS)]

    def right_copy(source, slot, which, step):
        return [
            pltpu.make_async_remote_copy(
                source.at[lines], right.at[slot - 1, lines], send_c.at[which, k], recv_c.at[slot - 1, k],
                device_id={"col": lax.rem(c + ncol + step, ncol)}, device_id_type=MESH,
            )
            for k, lines in enumerate(pieces)
        ]

    def left_copy(source, slot, sender, to):
        return pltpu.make_async_remote_copy(
            source, left.at[slot], sender, recv_l.at[slot], device_id={"row": to}, device_id_type=MESH
        )

    def slot_of(i):
        return lax.rem(c + ncol - (r * held + i), ncol)

    def own_copies(i):
        slot = jnp.minimum(slot_of(i), STEPS - 1)
        copies = []
        for d in range(1, nrow // 2):
            chip = lax.rem(lax.div(r, 2) + d, nrow // 2)
            copies.append(left_copy(send_left.at[i], slot, send_l.at[i, d], 2 * chip + lax.rem(i, 2)))
        copies.append(left_copy(send_left.at[i], slot, send_l.at[i, 0], other_core))
        return copies

    two_on = right_copy(send_right, 2, 0, 2)
    own_on = right_copy(send_right, 1, 1, 1)
    pass_back = right_copy(right.at[1], 1, 1, -1)
    pass_on = right_copy(right.at[1], 3, 2, 1)

    cut = FLAG_ROWS * (5 * (samples + FLAG_ROWS) // (6 * FLAG_ROWS) + 1)
    upper, lower, lower_here = slice(0, cut), slice(cut, samples + FLAG_ROWS), slice(0, samples + FLAG_ROWS - cut)

    def relay_copy(source, target, sender, receiver, step):
        return pltpu.make_async_remote_copy(
            source, target, send_relay.at[sender], receiver,
            device_id={"col": lax.rem(c + ncol + step, ncol)}, device_id_type=MESH,
        )

    upper_out = relay_copy(send_right.at[upper], relay.at[upper], 0, recv_relay.at[0], -1)
    lower_out = relay_copy(send_right.at[lower], relay.at[lower_here], 1, recv_relay.at[0], 4)
    upper_on = relay_copy(relay.at[upper], right.at[2, upper], 0, recv_c.at[2, 0], 4)
    lower_on = relay_copy(relay.at[lower_here], right.at[2, lower], 2, recv_c.at[2, 1], -1)
    for piece in two_on:
        piece.start()

    @pl.when(jnp.logical_not(even))
    def _():
        upper_out.start()
        lower_out.start()

    @pl.when(even)
    def _():
        for piece in own_on:
            piece.start()

    loads[2].wait()
    loads[3].wait()
    for i in range(held):
        flag = rv_here[i : i + 1, :].astype(jnp.float32)
        for j in range(tiles):
            block = rr_here[i, :, 128 * j : 128 * (j + 1)].astype(jnp.float32).T * flag
            send_left[i, 128 * j : 128 * (j + 1), :] = block.astype(jnp.bfloat16)
        send_left[i, samples:, :] = jnp.broadcast_to(flag, (FLAG_ROWS, rows)).astype(jnp.bfloat16)
    for k in range(held):
        i = lax.rem(c + k, held)

        @pl.when(slot_of(i) < STEPS)
        def _():
            for copy in own_copies(i):
                copy.start()
            left[jnp.minimum(slot_of(i), STEPS - 1)] = send_left[i]

    padded[:, 0:128] = jnp.zeros((cols, 128), jnp.bfloat16)
    padded[:, 128 + samples :] = jnp.zeros((cols, 128), jnp.bfloat16)
    shifted[0:FINE, :] = jnp.zeros((FINE, rows), jnp.float32)
    shifted[FINE + samples :, :] = jnp.zeros((FINE, rows), jnp.float32)

    def stack(p, source):
        target, begin_at = (stacked_a, p * samples) if p < STEPS - 1 else (stacked, 0)
        for j in range(tiles):
            padded[:, 128 * (j + 1) : 128 * (j + 2)] = source[128 * j : 128 * (j + 1), :]
        for h in range(coarse):
            begin = 128 + FINE * h - LAG
            lines = slice(h * cols, (h + 1) * cols)
            target[lines, begin_at : begin_at + samples] = padded[:, begin : begin + samples]
            stacked[lines, samples + p * FINE : samples + (p + 1) * FINE] = padded[:, begin + samples : begin + samples + FINE]

    def weigh(p, slot):
        target, begin_at = (weights_a, p * samples) if p < STEPS - 1 else (weights, 0)
        shifted[FINE : FINE + samples, :] = left[slot, 0:samples, :].astype(jnp.float32)
        for g in range(FINE):
            lanes = slice(g * rows, (g + 1) * rows)
            target[begin_at : begin_at + samples, lanes] = shifted[FINE - g : FINE - g + samples, :].astype(jnp.bfloat16)
            weights[samples + p * FINE : samples + (p + 1) * FINE, lanes] = shifted[
                FINE - g + samples : 2 * FINE - g + samples, :
            ].astype(jnp.bfloat16)

    def facts(s):
        window = lax.rem(c + ncol - s, ncol)
        owner = lax.div(window, held)
        passes = jnp.logical_and(
            lax.div(owner, 2) != lax.div(r, 2), lax.rem(lax.rem(window, held), 2) == lax.rem(r, 2)
        )
        return owner, passes

    def pass_copy(s):
        return left_copy(left.at[s], s, pass_l.at[s], other_core)

    def left_wait(s):
        owner, passes = facts(s)

        @pl.when(jnp.logical_and(owner != r, jnp.logical_not(passes)))
        def _():
            left_copy(send_left.at[0], s, pass_l.at[0], other_core).wait_recv()

    def right_wait(slot):
        for piece in right_copy(send_right, slot, 0, 2):
            piece.wait_recv()

    def multiply(first, last, add):
        for p in range(FINE // 2):
            for h in range(coarse):
                single = h == coarse - 1
                if single and p > 0:
                    continue
                width = rows if single else 2 * rows
                product = jnp.dot(
                    stacked_a[h * cols : (h + 1) * cols, first:last],
                    weights_a[first:last, 2 * p * rows : 2 * p * rows + width],
                    preferred_element_type=jnp.float32,
                )
                for q in range(width // rows):
                    lag = FINE * h + 2 * p + q
                    term = product[:, q * rows : (q + 1) * rows]
                    partial[lag] = partial[lag] + term if add else term

    def left_pass(s):
        owner, passes = facts(s)

        @pl.when(passes)
        def _():
            left_copy(send_left.at[0], s, pass_l.at[s], other_core).wait_recv()
            pass_copy(s).start()

    @pl.when(even)
    def _():
        upper_out.wait_recv()
        upper_on.start()

    def pairs(s):
        source = send_right if s == 0 else right.at[s - 1]
        col_flag = source[samples : samples + FLAG_ROWS, :].astype(jnp.float32)[0:1, :]
        row_flag = left[s, samples : samples + FLAG_ROWS, :].astype(jnp.float32)[0:1, :]
        return jnp.broadcast_to(col_flag, (cols, cols)).T * row_flag

    stack(0, send_right)
    left_pass(0)
    left_wait(0)
    weigh(0, 0)
    multiply(0, samples, False)

    for k in range(tiles):
        two_on[k].wait_recv()

        @pl.when(even)
        def _():
            pass_on[k].start()

        @pl.when(jnp.logical_not(even))
        def _():
            pass_back[k].start()

    @pl.when(jnp.logical_not(even))
    def _():
        lower_out.wait_recv()
        lower_on.start()

    for s in (2, 1, 3):
        left_pass(s)
    stack(1, right.at[1])
    left_wait(2)
    weigh(1, 2)
    multiply(samples, 2 * samples, True)
    left_wait(1)
    weigh(2, 1)
    right_wait(1)
    stack(2, right.at[0])
    multiply(2 * samples, 3 * samples, True)
    left_wait(3)
    weigh(3, 3)
    scale[...] = pairs(0) + pairs(1) + pairs(2)
    @pl.when(even)
    def _():
        upper_on.wait_recv()
        lower_on.wait_recv()

    @pl.when(jnp.logical_not(even))
    def _():
        right_wait(3)

    stack(3, right.at[2])
    count = scale[...] + pairs(3)
    scale[...] = 1.0 / (jnp.sqrt(jnp.float32(samples)) * jnp.maximum(count, 1.0))

    for piece in two_on + own_on:
        piece.wait_send()
    upper_out.wait_send()

    @pl.when(even)
    def _():
        for piece in pass_on:
            piece.wait_send()

    @pl.when(jnp.logical_not(even))
    def _():
        lower_out.wait_send()
        lower_on.wait_send()

    for i in range(held):
        @pl.when(slot_of(i) < STEPS)
        def _():
            for copy in own_copies(i):
                copy.wait_send()
    for s in range(STEPS):
        owner, passes = facts(s)

        @pl.when(passes)
        def _():
            pass_copy(s).wait_send()


def correlate_kernel(stacked, weights, partial, scale, out, result, sem):
    cols, rows = scale.shape
    coarse = stacked.shape[0] // cols
    copies = []
    for p in range(FINE // 2):
        for h in range(coarse):
            single = h == coarse - 1
            if single and p > 0:
                continue
            width = rows if single else 2 * rows
            product = jnp.dot(
                stacked[h * cols : (h + 1) * cols, :],
                weights[:, 2 * p * rows : 2 * p * rows + width],
                preferred_element_type=jnp.float32,
            )
            for q in range(width // rows):
                lag = FINE * h + 2 * p + q
                result[lag] = (partial[lag] + product[:, q * rows : (q + 1) * rows]) * scale[...]
                copy = pltpu.make_async_copy(result.at[lag], out.at[lag], sem.at[lag])
                copy.start()
                copies.append(copy)
    for copy in copies:
        copy.wait()


def shards(row_records, row_valid, col_records, col_valid):
    nrow = lax.axis_size("row")
    ncol = lax.axis_size("col")
    held, rows, samples = row_records.shape
    cols = col_records.shape[1]
    lags = 2 * LAG + 1
    coarse = 2 * LAG // FINE + 1
    early = (STEPS - 1) * samples
    late = samples + STEPS * FINE
    any_space = pl.BlockSpec(memory_space=pl.ANY)
    vmem = pl.BlockSpec(memory_space=pltpu.VMEM)
    dma = pltpu.SemaphoreType.DMA
    operands = pl.pallas_call(
        functools.partial(gather_kernel, nrow, ncol),
        out_shape=(
            jax.ShapeDtypeStruct((coarse * cols, late), jnp.bfloat16),
            jax.ShapeDtypeStruct((late, FINE * rows), jnp.bfloat16),
            jax.ShapeDtypeStruct((lags, cols, rows), jnp.float32),
            jax.ShapeDtypeStruct((cols, rows), jnp.float32),
        ),
        in_specs=[pl.BlockSpec(memory_space=pltpu.HBM)] * 4,
        out_specs=(vmem,) * 4,
        scratch_shapes=[
            pltpu.VMEM((coarse * cols, early), jnp.bfloat16),
            pltpu.VMEM((early, FINE * rows), jnp.bfloat16),
            pltpu.VMEM((held, rows, samples), jnp.bfloat16),
            pltpu.VMEM((held, rows), jnp.int32),
            pltpu.VMEM((1, cols, samples), jnp.bfloat16),
            pltpu.VMEM((1, cols), jnp.int32),
            pltpu.VMEM((held, samples + FLAG_ROWS, rows), jnp.bfloat16),
            pltpu.VMEM((samples + FLAG_ROWS, cols), jnp.bfloat16),
            pltpu.VMEM((STEPS, samples + FLAG_ROWS, rows), jnp.bfloat16),
            pltpu.VMEM((STEPS - 1, samples + FLAG_ROWS, cols), jnp.bfloat16),
            pltpu.VMEM((cols, samples + 256), jnp.bfloat16),
            pltpu.VMEM((samples + 2 * FINE, rows), jnp.float32),
            dma((4,)),
            dma((held, nrow // 2)),
            dma((STEPS,)),
            dma((STEPS,)),
            dma((STEPS - 1, samples // 128)),
            dma((STEPS - 1, samples // 128)),
            dma((3,)),
            dma((1,)),
            pltpu.VMEM((samples + FLAG_ROWS, cols), jnp.bfloat16),
        ],
        compiler_params=pltpu.CompilerParams(
            collective_id=0, has_side_effects=True, vmem_limit_bytes=20 * 1024 * 1024
        ),
        name="gather",
    )(*(pltpu.with_memory_space_constraint(x, pltpu.HBM) for x in (row_records, row_valid, col_records, col_valid)))
    return pl.pallas_call(
        correlate_kernel,
        out_shape=jax.ShapeDtypeStruct((lags, cols, rows), jnp.float32),
        in_specs=[vmem] * 4,
        out_specs=any_space,
        scratch_shapes=[pltpu.VMEM((lags, cols, rows), jnp.float32), dma((lags,))],
        compiler_params=pltpu.CompilerParams(vmem_limit_bytes=16 * 1024 * 1024),
        name="correlate",
    )(*operands)


def solution(mesh):
    return jax.shard_map(
        shards,
        mesh=mesh,
        in_specs=(P("row", "col", None), P("row", "col"), P("col", "row", None), P("col", "row")),
        out_specs=P(None, "row", "col"),
        check_vma=False,
    )
```
